32 devices in a mesh: row: 4 (over y, core), col: 8 (over z, x).
Axes of the slice: x: 2, y: 2, z: 4, core: 2. Of those that a mesh axis runs over, the one named last changes fastest.
Arguments:
- features: float32 [3072, 128], P(('row', 'col')), may hold values from -1 to 1
- solves: float32 [3072, 64], P(('row', 'col')), may hold values from -48 to 48
- probes: float32 [3072, 64], P(('row', 'col')), may hold values from -48 to 48
Outputs:
- gradient: float32 [3072, 128], P(('row', 'col'))
The draws below stay inside these ranges and needn't reach their ends.
All inputs are finite; a program needn't handle non-finite values.
Results may differ from the reference program's by a relative error of at most 0.0003.
Values sent between devices are 32-bit elements; how exact they have to be, the bound alone decides.
No kernel may reach another device: no remote copies, remote signals or barrier semaphores. Data moves between devices by JAX's collectives and lax.ppermute only.
A program may use at most 64 MiB of HBM per device.

```python
import jax
import jax.numpy as jnp
from jax import lax

F = 128
P_SIZE = 64
N = 3072


def draw_features(key, part):
    first_key = jax.random.fold_in(key, 0)
    spread = jnp.sqrt(jnp.float32(4.5) / jnp.float32(F))
    values = jax.random.normal(first_key, (N, F), jnp.float32) * spread
    return jnp.clip(values, -1.0, 1.0)


def block_levels(key, dims, shards, smallest, largest):
    def one(position, shards_of):
        heights = jax.random.uniform(jax.random.fold_in(jax.random.fold_in(key, 6), position), (shards_of,), jnp.float32, smallest / len(shards), largest / len(shards))
        return jnp.repeat(jnp.exp(heights), dims[position] // shards_of).reshape((-1,) + (1,) * (len(dims) - position - 1))

    level = one(*shards[0])
    for cut in shards[1:]:
        level = level * one(*cut)
    return level


def noise(rng, extent, scale, reach, cuts=(), held_as=jnp.bfloat16):
    result = scale * jax.random.normal(rng, extent, jnp.float32)
    if cuts:
        result = result * block_levels(rng, extent, cuts, -0.22, 0.18)
    return jnp.clip(result, -reach, reach).astype(held_as)


def setup_inputs(seed: int = 0) -> dict:
    arg_keys = jax.random.split(jax.random.key(seed), 4)
    features = draw_features(jax.random.fold_in(arg_keys[3], 71), 0)
    solves = noise(arg_keys[1], (N, P_SIZE), 8.0, 48.0, ((0, 32),), jnp.float32)
    probes = noise(arg_keys[2], (N, P_SIZE), 8.0, 48.0, ((0, 32),), jnp.float32)
    return dict(features=features, solves=solves, probes=probes)


HIGH = lax.Precision.HIGHEST

def reference(features, solves, probes):
    block = 2048 if N % 2048 == 0 else N
    sq_all = lax.optimization_barrier(jnp.sum(features * features, axis=1))

    def one_block(index):
        start = index * block
        rows_x = lax.dynamic_slice_in_dim(features, start, block, 0)
        rows_u = lax.dynamic_slice_in_dim(solves, start, block, 0)
        rows_v = lax.dynamic_slice_in_dim(probes, start, block, 0)
        rows_sq = lax.optimization_barrier(jnp.sum(rows_x * rows_x, axis=1))
        inner = jnp.dot(rows_x, features.T, precision=HIGH, preferred_element_type=jnp.float32)
        dist = rows_sq[:, None] + sq_all[None, :] - 2.0 * inner
        kernel = jnp.exp(-0.5 * dist)
        weight = jnp.dot(rows_u, probes.T, precision=HIGH, preferred_element_type=jnp.float32)
        weight = weight + jnp.dot(rows_v, solves.T, precision=HIGH, preferred_element_type=jnp.float32)
        coupling = kernel * weight
        mixed = jnp.dot(coupling, features, precision=HIGH, preferred_element_type=jnp.float32)
        totals = lax.optimization_barrier(jnp.sum(coupling, axis=1))
        scale = -2.0 / jnp.sqrt(jnp.float32(N) * jnp.float32(P_SIZE))
        return scale * (rows_x * totals[:, None] - mixed)
    parts = lax.map(one_block, jnp.arange(N // block, dtype=jnp.int32))
    return parts.reshape(N, F)
```

```python
import functools

import jax
import jax.numpy as jnp
from jax import lax
from jax.experimental import pallas as pl
from jax.experimental.pallas import tpu as pltpu
from jax.sharding import Mesh, PartitionSpec as P

NT = (((1,), (1,)), ((), ()))
NN = (((1,), (0,)), ((), ()))


def shifted(index, step, size):
    return index ^ step if size & (size - 1) == 0 else (index + step) % size


def send(block, axis, step, back=False):
    size = lax.axis_size(axis)
    pairs = [(i, shifted(i, step, size)) for i in range(size)]
    return lax.ppermute(block, axis, [(j, i) for i, j in pairs] if back else pairs)


def pieces(value, count):
    parts = []
    for _ in range(count):
        part = value.astype(jnp.bfloat16)
        parts.append(part)
        value = value - part.astype(jnp.float32)
    return parts


def product(left, right, dims):
    count = len(left)
    total = None
    for order in range(count - 1, -1, -1):
        for i in range(order + 1):
            term = lax.dot_general(left[i], right[order - i], dims, preferred_element_type=jnp.float32)
            total = term if total is None else total + term
    return total


def couple(features, scale, n_targets, n_sources, n_sums, *refs):
    targets = refs[:n_targets]
    sources = refs[n_targets : n_targets + n_sources]
    sums = refs[n_targets + n_sources : n_targets + n_sources + n_sums]
    outs = refs[n_targets + n_sources + n_sums :]
    source = jnp.concatenate([ref[...] for ref in sources], axis=0)
    xs, ws = source[:, :features], source[:, features:]
    half = ws.shape[1] // 2
    ws = jnp.concatenate([ws[:, half:], ws[:, :half]], axis=1)
    xs_pieces, ws_pieces = pieces(xs, 3), pieces(ws, 2)
    ones = jnp.ones((8, features), jnp.bfloat16)
    square_s = sum(lax.dot_general(ones, part, NT, preferred_element_type=jnp.float32) for part in reversed(pieces(xs * xs, 3)))[:1]
    group = n_targets // len(outs)
    for g, out in enumerate(outs):
        target = jnp.concatenate([ref[...] for ref in targets[g * group : (g + 1) * group]], axis=0)
        xt, wt = target[:, :features], target[:, features:]
        inner = product(pieces(xt, 3), xs_pieces, NT)
        dist = jnp.sum(xt * xt, axis=1, keepdims=True) + square_s - 2.0 * inner
        coupling = jnp.exp(-0.5 * dist) * product(pieces(wt, 2), ws_pieces, NT)
        totals = jnp.sum(coupling, axis=1, keepdims=True)
        mixed = product(pieces(coupling, 2), xs_pieces[:2], NN)
        value = scale * (xt * totals - mixed)
        out[...] = value + sums[g][...] if n_sums else value


def partial(features, scale, groups, sources, sums):
    targets = [block for group in groups for block in group]
    rows, width = targets[0].shape
    n_t, n_s = rows * len(targets), rows * len(sources)
    return pl.pallas_call(
        functools.partial(couple, features, scale, len(targets), len(sources), len(sums)),
        out_shape=[jax.ShapeDtypeStruct((rows * len(group), features), jnp.float32) for group in groups],
        in_specs=[pl.BlockSpec(memory_space=pltpu.VMEM)] * (len(targets) + len(sources) + len(sums)),
        out_specs=[pl.BlockSpec(memory_space=pltpu.VMEM)] * len(groups),
        cost_estimate=pl.CostEstimate(
            flops=24 * n_t * n_s * features, bytes_accessed=4 * (n_t + n_s) * width, transcendentals=n_t * n_s
        ),
        compiler_params=pltpu.CompilerParams(vmem_limit_bytes=48 * 1024 * 1024),
    )(*targets, *sources, *sums)


def local(total, features, solves, probes):
    width, vectors = features.shape[1], solves.shape[1]
    scale = -2.0 / (float(total) * float(vectors)) ** 0.5
    n_far, n_x, n_y = lax.axis_size("far"), lax.axis_size("x"), lax.axis_size("y")
    n_core = lax.axis_size("core")
    own = jnp.concatenate([features, solves, probes], axis=1)
    rows = own.shape[0]

    far = {step: send(own, "far", step) for step in range(n_far - 1, 0, -1)}
    beside = [own] + [send(own, "x", step) for step in range(1, n_x)]
    pair = jnp.concatenate(beside, axis=0)
    groups = [beside]
    for step in range(1, n_y):
        block = send(pair, "y", step)
        groups.append([block[i * rows : (i + 1) * rows] for i in range(n_x)])
    groups = [[groups[y][x] for y in range(n_y)] for x in range(n_x)]

    sums = []
    near = [own] + [send(own, "core", step) for step in range(1, n_core)]
    sums = partial(width, scale, groups, near, sums)
    for step in range(1, n_far):
        block = far[step]
        sources = [block] + [send(block, "core", other) for other in range(1, n_core)]
        sums = partial(width, scale, groups, sources, sums)

    column = sums[0]
    for step in range(1, n_x):
        column = column + send(sums[step], "x", step, back=True)
    out = column[:rows]
    for step in range(1, n_y):
        out = out + send(column[step * rows : (step + 1) * rows], "y", step, back=True)
    return out


def solution(mesh):
    n_row, n_col = mesh.shape["row"], mesh.shape["col"]
    n_core, n_x = (2 if n % 2 == 0 else 1 for n in (n_row, n_col))
    shape = (n_row // n_core, n_core, n_col // n_x, n_x)
    fine = Mesh(mesh.devices.reshape(shape), ("y", "core", "far", "x"))
    spec = P(("y", "core", "far", "x"), None)

    def run(features, solves, probes):
        inner = functools.partial(local, features.shape[0])
        return jax.shard_map(inner, mesh=fine, in_specs=(spec,) * 3, out_specs=spec, check_vma=False)(features, solves, probes)

    return run
```

```python
import functools
import itertools

import jax
import jax.numpy as jnp
from jax import lax
from jax.experimental import pallas as pl
from jax.experimental.pallas import tpu as pltpu
from jax.sharding import Mesh, PartitionSpec as P

NT = (((1,), (1,)), ((), ()))
NN = (((1,), (0,)), ((), ()))


def shifted(index, step, size):
    return index ^ step if size & (size - 1) == 0 else (index + step) % size


def send(block, axes, steps, back=False):
    sizes = [lax.axis_size(axis) for axis in axes]
    places = list(itertools.product(*map(range, sizes)))
    number = {place: i for i, place in enumerate(places)}
    pairs = [(number[place], number[tuple(map(shifted, place, steps, sizes))]) for place in places]
    return lax.ppermute(block, axes, [(j, i) for i, j in pairs] if back else pairs)


def pieces(value, count):
    parts = []
    for _ in range(count):
        part = value.astype(jnp.bfloat16)
        parts.append(part)
        value = value - part.astype(jnp.float32)
    return parts


def product(left, right, dims):
    terms = [(left[i], right[order - i]) for order in range(len(left)) for i in range(order + 1)]
    long_left, long_right = (jnp.concatenate(side, axis=axis[0]) for side, axis in zip(zip(*terms), dims[0]))
    return lax.dot_general(long_left, long_right, dims, preferred_element_type=jnp.float32)


def pack(features_ref, solves_ref, probes_ref, out_ref, both, sems):
    width, vectors = features_ref.shape[1], solves_ref.shape[0]
    copies = [
        pltpu.make_async_copy(solves_ref, both.at[:vectors], sems.at[0]),
        pltpu.make_async_copy(probes_ref, both.at[vectors:], sems.at[1]),
        pltpu.make_async_copy(features_ref, out_ref.at[:, :width], sems.at[2]),
    ]
    for copy in copies:
        copy.start()
    for copy in copies[:2]:
        copy.wait()
    out_ref[:, width:] = both[...].T
    copies[2].wait()


def packed(features, solves, probes):
    rows, width = features.shape[0], features.shape[1] + solves.shape[1] + probes.shape[1]
    return pl.pallas_call(
        pack,
        out_shape=pltpu.VMEM((rows, width), jnp.float32),
        in_specs=[pl.BlockSpec(memory_space=pltpu.HBM)] * 3,
        out_specs=pl.BlockSpec(memory_space=pltpu.VMEM),
        scratch_shapes=[
            pltpu.VMEM((solves.shape[1] + probes.shape[1], rows), jnp.float32),
            pltpu.SemaphoreType.DMA((3,)),
        ],
        compiler_params=pltpu.CompilerParams(vmem_limit_bytes=8 * 1024 * 1024),
    )(*(pltpu.with_memory_space_constraint(a, pltpu.HBM) for a in (features, solves.T, probes.T)))


def couple(features, scale, chunk, n_targets, n_sources, *refs):
    targets, sources, outs = refs[:n_targets], refs[n_targets : n_targets + n_sources], refs[n_targets + n_sources :]
    target = jnp.concatenate([ref[...] for ref in targets], axis=0)
    xt, wt = target[:, :features], target[:, features:]
    xt_pieces, wt_pieces = pieces(xt, 3), pieces(wt, 2)
    square_t = jnp.sum(xt * xt, axis=1, keepdims=True)
    ones = jnp.ones((8, features), jnp.bfloat16)
    totals, mixed = [], []
    for first in range(0, n_sources, chunk):
        source = jnp.concatenate([ref[...] for ref in sources[first : first + chunk]], axis=0)
        xs, ws = source[:, :features], source[:, features:]
        half = ws.shape[1] // 2
        ws = jnp.concatenate([ws[:, half:], ws[:, :half]], axis=1)
        xs_pieces = pieces(xs, 3)
        squares = [lax.dot_general(ones, part, NT, preferred_element_type=jnp.float32) for part in reversed(pieces(xs * xs, 3))]
        inner = product(xt_pieces, xs_pieces, NT)
        kernel = jnp.exp(inner - (0.5 * square_t + 0.5 * sum(squares)[:1]))
        coupling = kernel * product(wt_pieces, pieces(ws, 2), NT)
        totals.append(jnp.sum(coupling, axis=1, keepdims=True))
        mixed.append(product(pieces(coupling, 2), xs_pieces[:2], NN))
    value = scale * (xt * sum(totals) - sum(mixed))
    rows = outs[0].shape[0]
    for i, out in enumerate(outs):
        out[...] = value[i * rows : (i + 1) * rows]


def partial(features, scale, rows, targets, sources):
    n_t, n_s = (sum(block.shape[0] for block in blocks) for blocks in (targets, sources))
    chunk = min(4, len(sources))
    return pl.pallas_call(
        functools.partial(couple, features, scale, chunk, len(targets), len(sources)),
        out_shape=[jax.ShapeDtypeStruct((rows, features), jnp.float32) for _ in range(n_t // rows)],
        in_specs=[pl.BlockSpec(memory_space=pltpu.VMEM)] * (len(targets) + len(sources)),
        out_specs=[pl.BlockSpec(memory_space=pltpu.VMEM)] * (n_t // rows),
        cost_estimate=pl.CostEstimate(
            flops=24 * n_t * n_s * features, bytes_accessed=8 * (n_t + n_s) * features, transcendentals=n_t * n_s
        ),
        compiler_params=pltpu.CompilerParams(vmem_limit_bytes=32 * 1024 * 1024),
    )(*targets, *sources)


def local(total, features, solves, probes):
    width, vectors = features.shape[1], solves.shape[1]
    scale = -2.0 / (float(total) * float(vectors)) ** 0.5
    n_far, n_x, n_y = lax.axis_size("far"), lax.axis_size("x"), lax.axis_size("y")
    n_core = lax.axis_size("core")
    own = packed(features, solves, probes)

    def across(block):
        return [block] + [send(block, ("core",), (step,)) for step in range(1, n_core)]

    near = across(own)
    places = list(itertools.product(range(n_y), range(n_x)))
    far = [send(own, ("far",), (step,)) for step in range(n_far - 1, 0, -1)]
    gate = own
    beside = [own] + [send(gate, ("x",), (step,)) for step in range(1, n_x)]
    pair = jnp.concatenate(beside, axis=0)
    targets = beside + [send(pair, ("y",), (step,)) for step in range(1, n_y)]
    sources = near + [part for block in far for part in across(block)]
    sums = partial(width, scale, own.shape[0], targets, sources)

    out = sums[0]
    for place, part in zip(places[1:], sums[1:], strict=True):
        out = out + send(part, ("y", "x"), place, back=True)
    return out


def solution(mesh):
    n_row, n_col = mesh.shape["row"], mesh.shape["col"]
    n_core, n_x = (2 if n % 2 == 0 else 1 for n in (n_row, n_col))
    shape = (n_row // n_core, n_core, n_col // n_x, n_x)
    fine = Mesh(mesh.devices.reshape(shape), ("y", "core", "far", "x"))
    spec = P(("y", "core", "far", "x"), None)

    def run(features, solves, probes):
        inner = functools.partial(local, features.shape[0])
        return jax.shard_map(inner, mesh=fine, in_specs=(spec,) * 3, out_specs=spec, check_vma=False)(features, solves, probes)

    return run
```

```python
import functools
import itertools

import jax
import jax.numpy as jnp
from jax import lax
from jax.experimental import pallas as pl
from jax.experimental.pallas import tpu as pltpu
from jax.sharding import Mesh, PartitionSpec as P

NT = (((1,), (1,)), ((), ()))
NN = (((1,), (0,)), ((), ()))


def shifted(index, step, size):
    return index ^ step if size & (size - 1) == 0 else (index + step) % size


def send(block, axes, steps, back=False):
    sizes = [lax.axis_size(axis) for axis in axes]
    places = list(itertools.product(*map(range, sizes)))
    number = {place: i for i, place in enumerate(places)}
    pairs = [(number[place], number[tuple(map(shifted, place, steps, sizes))]) for place in places]
    return lax.ppermute(block, axes, [(j, i) for i, j in pairs] if back else pairs)


def pieces(value, count):
    parts = []
    for _ in range(count):
        part = value.astype(jnp.bfloat16)
        parts.append(part)
        value = value - part.astype(jnp.float32)
    return parts


def product(left, right, dims):
    terms = [(left[i], right[order - i]) for order in range(len(left)) for i in range(order + 1)]
    long_left, long_right = (jnp.concatenate(side, axis=axis[0]) for side, axis in zip(zip(*terms), dims[0]))
    return lax.dot_general(long_left, long_right, dims, preferred_element_type=jnp.float32)


def pack(features_ref, solves_ref, probes_ref, out_ref, both, sems):
    width, vectors = features_ref.shape[1], solves_ref.shape[0]
    copies = [
        pltpu.make_async_copy(solves_ref, both.at[:vectors], sems.at[0]),
        pltpu.make_async_copy(probes_ref, both.at[vectors:], sems.at[1]),
        pltpu.make_async_copy(features_ref, out_ref.at[:, :width], sems.at[2]),
    ]
    for copy in copies:
        copy.start()
    for copy in copies[:2]:
        copy.wait()
    out_ref[:, width:] = both[...].T
    copies[2].wait()


def packed(features, solves, probes):
    rows, width = features.shape[0], features.shape[1] + solves.shape[1] + probes.shape[1]
    return pl.pallas_call(
        pack,
        out_shape=pltpu.VMEM((rows, width), jnp.float32),
        in_specs=[pl.BlockSpec(memory_space=pltpu.HBM)] * 3,
        out_specs=pl.BlockSpec(memory_space=pltpu.VMEM),
        scratch_shapes=[
            pltpu.VMEM((solves.shape[1] + probes.shape[1], rows), jnp.float32),
            pltpu.SemaphoreType.DMA((3,)),
        ],
        compiler_params=pltpu.CompilerParams(vmem_limit_bytes=8 * 1024 * 1024),
    )(*(pltpu.with_memory_space_constraint(a, pltpu.HBM) for a in (features, solves.T, probes.T)))


def couple(features, scale, counts, *refs):
    targets, sources, sums, outs = (refs[sum(counts[:i]) : sum(counts[: i + 1])] for i in range(4))
    target = jnp.concatenate([ref[...] for ref in targets], axis=0)
    source = jnp.concatenate([ref[...] for ref in sources], axis=0)
    xt, wt = target[:, :features], target[:, features:]
    xs, ws = source[:, :features], source[:, features:]
    half = ws.shape[1] // 2
    ws = jnp.concatenate([ws[:, half:], ws[:, :half]], axis=1)
    xs_pieces = pieces(xs, 3)
    square_t = jnp.sum(xt * xt, axis=1, keepdims=True)
    ones = jnp.ones((8, features), jnp.bfloat16)
    squares = [lax.dot_general(ones, part, NT, preferred_element_type=jnp.float32) for part in reversed(pieces(xs * xs, 3))]
    inner = product(pieces(xt, 3), xs_pieces, NT)
    kernel = jnp.exp(inner - (0.5 * square_t + 0.5 * sum(squares)[:1]))
    coupling = kernel * product(pieces(wt, 2), pieces(ws, 2), NT)
    totals = jnp.sum(coupling, axis=1, keepdims=True)
    upper, lower = xs_pieces[:2]
    right = jnp.concatenate(
        [jnp.concatenate([upper, lower], axis=1), jnp.concatenate([upper, jnp.zeros_like(lower)], axis=1)], axis=0
    )
    both = lax.dot_general(jnp.concatenate(pieces(coupling, 2), axis=1), right, NN, preferred_element_type=jnp.float32)
    value = scale * (xt * totals - (both[:, :features] + both[:, features:]))
    rows = outs[0].shape[0]
    for i, out in enumerate(outs):
        part = value[i * rows : (i + 1) * rows]
        out[...] = part + sums[i][...] if sums else part


def partial(features, scale, rows, targets, sources, sums=()):
    n_t, n_s = (sum(block.shape[0] for block in blocks) for blocks in (targets, sources))
    return pl.pallas_call(
        functools.partial(couple, features, scale, (len(targets), len(sources), len(sums), n_t // rows)),
        out_shape=[jax.ShapeDtypeStruct((rows, features), jnp.float32) for _ in range(n_t // rows)],
        in_specs=[pl.BlockSpec(memory_space=pltpu.VMEM)] * (len(targets) + len(sources) + len(sums)),
        out_specs=[pl.BlockSpec(memory_space=pltpu.VMEM)] * (n_t // rows),
        cost_estimate=pl.CostEstimate(
            flops=24 * n_t * n_s * features, bytes_accessed=8 * (n_t + n_s) * features, transcendentals=n_t * n_s
        ),
        compiler_params=pltpu.CompilerParams(vmem_limit_bytes=32 * 1024 * 1024),
    )(*targets, *sources, *sums)


def local(total, features, solves, probes):
    width, vectors = features.shape[1], solves.shape[1]
    scale = -2.0 / (float(total) * float(vectors)) ** 0.5
    n_far, n_x, n_y = lax.axis_size("far"), lax.axis_size("x"), lax.axis_size("y")
    n_core = lax.axis_size("core")
    own = packed(features, solves, probes)

    def across(block):
        return [block] + [send(block, ("core",), (step,)) for step in range(1, n_core)]

    near = across(own)
    places = list(itertools.product(range(n_y), range(n_x)))
    far = [send(own, ("far",), (step,)) for step in sorted(range(1, n_far), key=lambda step: (step != n_far // 2, step))]
    gate = own
    beside = [own] + [send(gate, ("x",), (step,)) for step in range(1, n_x)]
    pair = jnp.concatenate(beside, axis=0)
    targets = beside + [send(pair, ("y",), (step,)) for step in range(1, n_y)]
    sources = near + [part for block in far for part in across(block)]
    sums = partial(width, scale, own.shape[0], targets, sources)
    order = sorted(range(1, len(places)), key=lambda i: places[i][1] == 0)
    returned = [send(sums[i], ("y", "x"), places[i], back=True) for i in order]
    out = sums[0]
    for part in returned:
        out = out + part
    return out


def solution(mesh):
    n_row, n_col = mesh.shape["row"], mesh.shape["col"]
    n_core, n_x = (2 if n % 2 == 0 else 1 for n in (n_row, n_col))
    shape = (n_row // n_core, n_core, n_col // n_x, n_x)
    fine = Mesh(mesh.devices.reshape(shape), ("y", "core", "far", "x"))
    spec = P(("y", "core", "far", "x"), None)

    def run(features, solves, probes):
        inner = functools.partial(local, features.shape[0])
        return jax.shard_map(inner, mesh=fine, in_specs=(spec,) * 3, out_specs=spec, check_vma=False)(features, solves, probes)

    return run
```

```python
import functools
import itertools

import jax
import jax.numpy as jnp
from jax import lax
from jax.experimental import pallas as pl
from jax.experimental.pallas import tpu as pltpu
from jax.sharding import Mesh, PartitionSpec as P

NT = (((1,), (1,)), ((), ()))
NN = (((1,), (0,)), ((), ()))


def shifted(index, step, size):
    return index ^ step if size & (size - 1) == 0 else (index + step) % size


def send(block, axes, steps, back=False):
    sizes = [lax.axis_size(axis) for axis in axes]
    places = list(itertools.product(*map(range, sizes)))
    number = {place: i for i, place in enumerate(places)}
    pairs = [(number[place], number[tuple(map(shifted, place, steps, sizes))]) for place in places]
    return lax.ppermute(block, axes, [(j, i) for i, j in pairs] if back else pairs)


def pieces(value, count):
    parts = []
    for _ in range(count):
        part = value.astype(jnp.bfloat16)
        parts.append(part)
        value = value - part.astype(jnp.float32)
    return parts


def product(left, right):
    long_left = jnp.concatenate([part for part in left for _ in right], axis=1)
    long_right = jnp.concatenate([part for _ in left for part in right], axis=1)
    return lax.dot_general(long_left, long_right, NT, preferred_element_type=jnp.float32)


def pack(features_ref, solves_ref, probes_ref, out_ref, both, sems):
    width, vectors = features_ref.shape[1], solves_ref.shape[0]
    copies = [
        pltpu.make_async_copy(solves_ref, both.at[:vectors], sems.at[0]),
        pltpu.make_async_copy(probes_ref, both.at[vectors:], sems.at[1]),
        pltpu.make_async_copy(features_ref, out_ref.at[:, :width], sems.at[2]),
    ]
    for copy in copies:
        copy.start()
    for copy in copies[:2]:
        copy.wait()
    out_ref[:, width:] = both[...].T
    copies[2].wait()


def packed(features, solves, probes):
    rows, width = features.shape[0], features.shape[1] + solves.shape[1] + probes.shape[1]
    return pl.pallas_call(
        pack,
        out_shape=pltpu.VMEM((rows, width), jnp.float32),
        in_specs=[pl.BlockSpec(memory_space=pltpu.HBM)] * 3,
        out_specs=pl.BlockSpec(memory_space=pltpu.VMEM),
        scratch_shapes=[
            pltpu.VMEM((solves.shape[1] + probes.shape[1], rows), jnp.float32),
            pltpu.SemaphoreType.DMA((3,)),
        ],
        compiler_params=pltpu.CompilerParams(vmem_limit_bytes=8 * 1024 * 1024),
    )(*(pltpu.with_memory_space_constraint(a, pltpu.HBM) for a in (features, solves.T, probes.T)))


def couple(features, scale, counts, *refs):
    targets, sources, sums, outs = (refs[sum(counts[:i]) : sum(counts[: i + 1])] for i in range(4))
    target = jnp.concatenate([ref[...] for ref in targets], axis=0)
    source = jnp.concatenate([ref[...] for ref in sources], axis=0)
    xt, wt = target[:, :features], target[:, features:]
    xs, ws = source[:, :features], source[:, features:]
    half = ws.shape[1] // 2
    ws = jnp.concatenate([ws[:, half:], ws[:, :half]], axis=1)
    xs_pieces = pieces(xs, 2)
    square_t = jnp.sum(xt * xt, axis=1, keepdims=True)
    ones = jnp.ones((8, features), jnp.bfloat16)
    squares = [lax.dot_general(ones, part, NT, preferred_element_type=jnp.float32) for part in reversed(pieces(xs * xs, 3))]
    inner = product(pieces(xt, 2), xs_pieces)
    kernel = jnp.exp(inner - (0.5 * square_t + 0.5 * sum(squares)[:1]))
    coupling = kernel * product(pieces(wt, 2), pieces(ws, 2))
    totals = jnp.sum(coupling, axis=1, keepdims=True)
    upper, lower = xs_pieces
    right = jnp.concatenate(
        [jnp.concatenate([upper, lower], axis=1), jnp.concatenate([upper, jnp.zeros_like(lower)], axis=1)], axis=0
    )
    both = lax.dot_general(jnp.concatenate(pieces(coupling, 2), axis=1), right, NN, preferred_element_type=jnp.float32)
    value = scale * (xt * totals - (both[:, :features] + both[:, features:]))
    rows = outs[0].shape[0]
    for i, out in enumerate(outs):
        part = value[i * rows : (i + 1) * rows]
        out[...] = part + sums[i][...] if sums else part


def partial(features, scale, rows, targets, sources, sums=()):
    n_t, n_s = (sum(block.shape[0] for block in blocks) for blocks in (targets, sources))
    return pl.pallas_call(
        functools.partial(couple, features, scale, (len(targets), len(sources), len(sums), n_t // rows)),
        out_shape=[jax.ShapeDtypeStruct((rows, features), jnp.float32) for _ in range(n_t // rows)],
        in_specs=[pl.BlockSpec(memory_space=pltpu.VMEM)] * (len(targets) + len(sources) + len(sums)),
        out_specs=[pl.BlockSpec(memory_space=pltpu.VMEM)] * (n_t // rows),
        cost_estimate=pl.CostEstimate(
            flops=24 * n_t * n_s * features, bytes_accessed=8 * (n_t + n_s) * features, transcendentals=n_t * n_s
        ),
        compiler_params=pltpu.CompilerParams(vmem_limit_bytes=32 * 1024 * 1024),
    )(*targets, *sources, *sums)


def local(total, features, solves, probes):
    width, vectors = features.shape[1], solves.shape[1]
    scale = -2.0 / (float(total) * float(vectors)) ** 0.5
    n_far, n_x, n_y = lax.axis_size("far"), lax.axis_size("x"), lax.axis_size("y")
    n_core = lax.axis_size("core")
    own = packed(features, solves, probes)

    def across(block):
        return [block] + [send(block, ("core",), (step,)) for step in range(1, n_core)]

    near = across(own)
    places = list(itertools.product(range(n_y), range(n_x)))
    far = [send(own, ("far",), (step,)) for step in sorted(range(1, n_far), key=lambda step: (step != n_far // 2, step))]
    gate = own
    beside = [own] + [send(gate, ("x",), (step,)) for step in range(1, n_x)]
    pair = jnp.concatenate(beside, axis=0)
    targets = beside + [send(pair, ("y",), (step,)) for step in range(1, n_y)]
    sources = near + [part for block in far for part in across(block)]
    sums = partial(width, scale, own.shape[0], targets, sources)
    order = sorted(range(1, len(places)), key=lambda i: places[i][1] == 0)
    returned = [send(sums[i], ("y", "x"), places[i], back=True) for i in order]
    out = sums[0]
    for part in returned:
        out = out + part
    return out


def solution(mesh):
    n_row, n_col = mesh.shape["row"], mesh.shape["col"]
    n_core, n_x = (2 if n % 2 == 0 else 1 for n in (n_row, n_col))
    shape = (n_row // n_core, n_core, n_col // n_x, n_x)
    fine = Mesh(mesh.devices.reshape(shape), ("y", "core", "far", "x"))
    spec = P(("y", "core", "far", "x"), None)

    def run(features, solves, probes):
        inner = functools.partial(local, features.shape[0])
        return jax.shard_map(inner, mesh=fine, in_specs=(spec,) * 3, out_specs=spec, check_vma=False)(features, solves, probes)

    return run
```
